512 devices in a mesh: dp: 128 (over y, z_hi, x), rows: 4 (over z_lo, core).
Axes of the slice: x: 4, y: 8, z: 8 (z_hi: 4, z_lo: 2; z = z_hi * 2 + z_lo), core: 2. Of those that a mesh axis runs over, the one named last changes fastest.
Arguments:
- image_rows: bfloat16 [65536, 1152], P(('dp', 'rows')), may hold values from -1.0234375 to 1.0234375
- text_rows: bfloat16 [65536, 1152], P(('dp', 'rows')), may hold values from -1.0234375 to 1.0234375
- logit_scale: float32 [1], replicated, may hold values from 1 to 3
- logit_bias: float32 [1], replicated, may hold values from -3 to -1
Outputs:
- grad_image: bfloat16 [65536, 1152], P(('dp', 'rows'))
- grad_text: bfloat16 [65536, 1152], P(('dp', 'rows'))
The draws below stay inside these ranges and needn't reach their ends.
All inputs are finite; a program needn't handle non-finite values.
Results may differ from the reference program's by a relative error of at most 0.015.
Values may be sent and summed in bfloat16 or wider, within the bound.
A program may use at most 64 MiB of HBM per device.

```python
import math
import jax
import jax.numpy as jnp
from jax import lax

D = 1152
TOK_DEV = 128
TOKENS = 65536
N_DP = 128
N_ROWS = 4


def level_of(rng, shape, cuts, low, largest):
    gain, own = 1.0, jax.random.fold_in(rng, 6)
    for position, shards_of in cuts:
        steps = jnp.exp(jax.random.uniform(jax.random.fold_in(own, position), (shards_of,), jnp.float32, low / len(cuts), largest / len(cuts)))
        gain = gain * jnp.repeat(steps, shape[position] // shards_of).reshape([-1 if axis == position else 1 for axis in range(len(shape))])
    return gain


def noise(key, dims, spread, limit, pieces=(), kind=jnp.bfloat16):
    level = level_of(key, dims, pieces, -0.22, 0.18) if pieces else 1.0
    array = jax.random.normal(key, dims, jnp.float32) * spread * level
    return jnp.minimum(jnp.maximum(array, -limit), limit).astype(kind)


def setup_inputs(seed: int = 0) -> dict:
    key_of = jax.random.split(jax.random.key(seed), 5)
    image_rows = noise(key_of[0], (TOKENS, D), (D ** -0.25), 1.0234375, ((0, 512),))
    text_rows = noise(key_of[1], (TOKENS, D), (D ** -0.25), 1.0234375, ((0, 512),))
    logit_scale = jnp.clip(jnp.exp(jax.random.uniform(key_of[2], (1,), jnp.float32, math.log(1.0), math.log(3.0))), 1.0, 3.0)
    logit_bias = jnp.clip(jax.random.uniform(key_of[3], (1,), jnp.float32, -3.0, -1.0), -3.0, -1.0)
    return {"image_rows": image_rows, "text_rows": text_rows, "logit_scale": logit_scale, "logit_bias": logit_bias}


def weight_block(image_block, text_block, temper, offset, own_round, group_rows):
    logits = temper * jnp.dot(image_block, text_block.T, preferred_element_type=jnp.float32) + offset
    weights = jax.nn.sigmoid(logits)
    if own_round:
        weights = weights - jnp.eye(group_rows, dtype=jnp.float32)
    return weights.astype(jnp.bfloat16)

def reference(image_rows, text_rows, logit_scale, logit_bias):
    group_rows = TOK_DEV * N_ROWS
    quarter = N_DP // 4
    temper = logit_scale[0]
    offset = logit_bias[0]
    image_blocks = image_rows.reshape(N_DP, group_rows, D)
    text_blocks = text_rows.reshape(N_DP, group_rows, D)

    def image_grad(group_index):
        image_block = image_blocks[group_index]
        summed = jnp.zeros((group_rows, D), jnp.float32)
        for round_index in range(4):
            partner = jnp.bitwise_xor(group_index, jnp.int32(round_index * quarter))
            text_block = text_blocks[partner]
            weights = weight_block(image_block, text_block, temper, offset, round_index == 0, group_rows)
            summed = summed + jnp.dot(weights, text_block, preferred_element_type=jnp.float32)
        return (temper * summed).astype(jnp.bfloat16)

    def text_grad(owner_index):
        text_block = text_blocks[owner_index]
        summed = jnp.zeros((group_rows, D), jnp.float32)
        for round_index in range(4):
            source = jnp.bitwise_xor(owner_index, jnp.int32(round_index * quarter))
            image_block = image_blocks[source]
            weights = weight_block(image_block, text_block, temper, offset, round_index == 0, group_rows)
            partial_terms = temper * jnp.einsum('rac,rad->rcd', weights.reshape(N_ROWS, TOK_DEV, group_rows).astype(jnp.float32), image_block.reshape(N_ROWS, TOK_DEV, D).astype(jnp.float32))
            rounded = lax.optimization_barrier(partial_terms.astype(jnp.bfloat16))
            summed = summed + lax.optimization_barrier(jnp.sum(rounded.astype(jnp.float32), axis=0))
        return summed.astype(jnp.bfloat16)
    indices = jnp.arange(N_DP, dtype=jnp.int32)
    grad_image = lax.map(image_grad, indices).reshape(N_DP * group_rows, D)
    grad_text = lax.map(text_grad, indices).reshape(N_DP * group_rows, D)
    return (grad_image, grad_text)
```

```python
import functools

import jax
import jax.numpy as jnp
from jax import lax
from jax.experimental import pallas as pl
from jax.experimental.pallas import tpu as pltpu
from jax.sharding import PartitionSpec as P

MESH = pl.DeviceIdType.MESH
CHUNKS = 4
F32 = jnp.float32
BF16 = jnp.bfloat16

I_CORE, I_Y, I_FWD, T_Z, T_Y, T_FWD = range(6)


def sigmoid(x):
    return 1.0 / (1.0 + jnp.exp(-x))


def kernel(
    quarter, rows, scale_ref, bias_ref, image_ref, text_ref, grad_image_ref, grad_text_ref,
    images, texts, weights, image_acc, text_acc, out_bf, staged, landed,
    send_sem, recv_sem, back_send, back_recv, local_sem, out_sem,
):
    dp, row = lax.axis_index("dp"), lax.axis_index("rows")
    low = quarter - 2 * quarter * ((dp // quarter) % 2)
    high = 2 * quarter - 4 * quarter * ((dp // (2 * quarter)) % 2)
    to_y2 = {"dp": dp + low, "rows": row}
    to_y6 = {"dp": dp + low + high, "rows": row}
    to_core = {"dp": dp, "rows": row + 1 - 2 * (row % 2)}
    to_z = {"dp": dp, "rows": row + 2 - 4 * (row // 2)}
    partner = {I_CORE: to_core, I_Y: to_y2, I_FWD: to_core, T_Z: to_z, T_Y: to_y6, T_FWD: to_z}
    part = rows // CHUNKS

    load_i = pltpu.make_async_copy(image_ref, images.at[pl.ds(0, rows)], local_sem.at[0])
    load_t = pltpu.make_async_copy(text_ref, texts.at[pl.ds(0, rows)], local_sem.at[1])
    load_i.start()
    load_t.start()
    barrier = pltpu.get_barrier_semaphore()
    for other in (to_y2, to_y6, to_core, to_z):
        pl.semaphore_signal(barrier, inc=1, device_id=other, device_id_type=MESH)
    pl.semaphore_wait(barrier, 4)
    load_i.wait()
    load_t.wait()

    def gather(stream, k):
        held = images if stream < T_Z else texts
        source = {I_CORE: 0, I_Y: 0, I_FWD: 2, T_Z: 0, T_Y: 0, T_FWD: 2}[stream]
        target = {I_CORE: 1, I_Y: 2, I_FWD: 3, T_Z: 1, T_Y: 2, T_FWD: 3}[stream]
        return pltpu.make_async_remote_copy(
            src_ref=held.at[pl.ds(source * rows + k * part, part)],
            dst_ref=held.at[pl.ds(target * rows + k * part, part)],
            send_sem=send_sem.at[stream, k],
            recv_sem=recv_sem.at[stream, k],
            device_id=partner[stream],
            device_id_type=MESH,
        )

    def back(stream, k):
        return pltpu.make_async_remote_copy(
            src_ref=staged.at[stream, pl.ds(k * part, part)],
            dst_ref=landed.at[stream, pl.ds(k * part, part)],
            send_sem=back_send.at[stream, k],
            recv_sem=back_recv.at[stream, k],
            device_id=partner[stream],
            device_id_type=MESH,
        )

    scale = scale_ref[0]
    bias = bias_ref[0]

    def fill_weights(i0, i1, t0, t1):
        block = lax.dot_general(
            images[pl.ds(i0 * rows, (i1 - i0) * rows)],
            texts[pl.ds(t0 * rows, (t1 - t0) * rows)],
            (((1,), (1,)), ((), ())),
            preferred_element_type=F32,
        )
        block = sigmoid(scale * block + bias)
        if i0 == 0 and t0 == 0:
            r = lax.broadcasted_iota(jnp.int32, block.shape, 0)
            c = lax.broadcasted_iota(jnp.int32, block.shape, 1)
            block = block - jnp.where((r == c) & (r < rows), 1.0, 0.0)
        weights[pl.ds(i0 * rows, (i1 - i0) * rows), pl.ds(t0 * rows, (t1 - t0) * rows)] = block.astype(BF16)

    def image_grad(i):
        return scale * jnp.dot(weights[pl.ds(i * rows, rows), :], texts[...], preferred_element_type=F32)

    def text_grad(t):
        return scale * lax.dot_general(
            weights[:, pl.ds(t * rows, rows)], images[...], (((0,), (0,)), ((), ())), preferred_element_type=F32
        )

    for k in range(CHUNKS):
        gather(I_Y, k).start()
        gather(T_Y, k).start()
        gather(T_Z, k).start()
        gather(I_CORE, k).start()
    for k in range(CHUNKS):
        gather(I_Y, k).wait_recv()
        gather(I_FWD, k).start()
        gather(T_Y, k).wait_recv()
        gather(T_FWD, k).start()
        if k == CHUNKS - 2:
            for j in range(CHUNKS):
                gather(I_CORE, j).wait_recv()
                gather(T_Z, j).wait_recv()
            fill_weights(0, 2, 0, 2)
    for k in range(CHUNKS):
        gather(I_FWD, k).wait_recv()
    fill_weights(2, 4, 0, 2)
    for k in range(CHUNKS):
        gather(T_FWD, k).wait_recv()
    fill_weights(0, 4, 2, 4)

    staged[T_FWD] = text_grad(3).astype(BF16)
    for k in range(CHUNKS):
        back(T_FWD, k).start()
    staged[I_FWD] = image_grad(3).astype(BF16)
    for k in range(CHUNKS):
        back(I_FWD, k).start()
    image_acc[...] = image_grad(2)
    for k in range(CHUNKS):
        back(I_FWD, k).wait_recv()
        at = pl.ds(k * part, part)
        staged[I_Y, at] = (image_acc[at] + landed[I_FWD, at].astype(F32)).astype(BF16)
        back(I_Y, k).start()
    text_acc[...] = text_grad(2)
    staged[T_Z] = text_grad(1).astype(BF16)
    for k in range(CHUNKS):
        back(T_FWD, k).wait_recv()
        at = pl.ds(k * part, part)
        staged[T_Y, at] = (text_acc[at] + landed[T_FWD, at].astype(F32)).astype(BF16)
        back(T_Y, k).start()
        back(T_Z, k).start()
    staged[I_CORE] = image_grad(1).astype(BF16)
    for k in range(CHUNKS):
        back(I_CORE, k).start()
    image_acc[...] = image_grad(0)
    text_acc[...] = text_grad(0)
    for k in range(CHUNKS):
        at = pl.ds(k * part, part)
        back(I_CORE, k).wait_recv()
        back(T_Z, k).wait_recv()
        image_acc[at] = image_acc[at] + landed[I_CORE, at].astype(F32)
        text_acc[at] = text_acc[at] + landed[T_Z, at].astype(F32)
    for k in range(CHUNKS):
        at = pl.ds(k * part, part)
        back(I_Y, k).wait_recv()
        out_bf[0, at] = (image_acc[at] + landed[I_Y, at].astype(F32)).astype(BF16)
        pltpu.make_async_copy(out_bf.at[0, at], grad_image_ref.at[at], out_sem.at[0, k]).start()
        back(T_Y, k).wait_recv()
        out_bf[1, at] = (text_acc[at] + landed[T_Y, at].astype(F32)).astype(BF16)
        pltpu.make_async_copy(out_bf.at[1, at], grad_text_ref.at[at], out_sem.at[1, k]).start()
    for stream in range(6):
        for k in range(CHUNKS):
            gather(stream, k).wait_send()
            back(stream, k).wait_send()
    for k in range(CHUNKS):
        at = pl.ds(k * part, part)
        pltpu.make_async_copy(out_bf.at[0, at], grad_image_ref.at[at], out_sem.at[0, k]).wait()
        pltpu.make_async_copy(out_bf.at[1, at], grad_text_ref.at[at], out_sem.at[1, k]).wait()


def per_device(image_rows, text_rows, logit_scale, logit_bias):
    rows, width = image_rows.shape
    quarter = lax.axis_size("dp") // 4
    shape = jax.ShapeDtypeStruct((rows, width), BF16)
    smem = pl.BlockSpec(memory_space=pltpu.SMEM)
    hbm = pl.BlockSpec(memory_space=pl.ANY)
    dma = pltpu.SemaphoreType.DMA
    return pl.pallas_call(
        functools.partial(kernel, quarter, rows),
        out_shape=(shape, shape),
        in_specs=[smem, smem, hbm, hbm],
        out_specs=(hbm, hbm),
        scratch_shapes=[
            pltpu.VMEM((4 * rows, width), BF16),
            pltpu.VMEM((4 * rows, width), BF16),
            pltpu.VMEM((4 * rows, 4 * rows), BF16),
            pltpu.VMEM((rows, width), F32),
            pltpu.VMEM((rows, width), F32),
            pltpu.VMEM((2, rows, width), BF16),
            pltpu.VMEM((6, rows, width), BF16),
            pltpu.VMEM((6, rows, width), BF16),
            dma((6, CHUNKS)),
            dma((6, CHUNKS)),
            dma((6, CHUNKS)),
            dma((6, CHUNKS)),
            dma((2,)),
            dma((2, CHUNKS)),
        ],
        compiler_params=pltpu.CompilerParams(
            collective_id=0, has_side_effects=True, vmem_limit_bytes=48 * 1024 * 1024
        ),
        cost_estimate=pl.CostEstimate(
            flops=6 * rows * rows * 16 * width, bytes_accessed=8 * rows * width, transcendentals=16 * rows * rows
        ),
        name="contrastive",
    )(logit_scale, logit_bias, image_rows, text_rows)


def solution(mesh):
    split = P(("dp", "rows"), None)
    return jax.shard_map(
        per_device,
        mesh=mesh,
        in_specs=(split, split, P(), P()),
        out_specs=(split, split),
        check_vma=False,
    )
```

```python
import functools

import jax
import jax.numpy as jnp
from jax import lax
from jax.experimental import pallas as pl
from jax.experimental.pallas import tpu as pltpu
from jax.sharding import PartitionSpec as P

MESH = pl.DeviceIdType.MESH
CHUNKS = 4
F32 = jnp.float32
BF16 = jnp.bfloat16

I_CORE, I_Y, I_FWD, T_Z, T_Y, T_FWD = range(6)


def sigmoid(x):
    return 1.0 / (1.0 + jnp.exp(-x))


def kernel(
    quarter, rows, scale_ref, bias_ref, image_ref, text_ref, grad_image_ref, grad_text_ref,
    images, texts, weights, image_acc, text_acc, staged, landed,
    send_sem, recv_sem, back_send, back_recv, local_sem,
):
    dp, row = lax.axis_index("dp"), lax.axis_index("rows")
    low = quarter - 2 * quarter * ((dp // quarter) % 2)
    high = 2 * quarter - 4 * quarter * ((dp // (2 * quarter)) % 2)
    to_y2 = {"dp": dp + low, "rows": row}
    to_y6 = {"dp": dp + low + high, "rows": row}
    to_core = {"dp": dp, "rows": row + 1 - 2 * (row % 2)}
    to_z = {"dp": dp, "rows": row + 2 - 4 * (row // 2)}
    partner = {I_CORE: to_core, I_Y: to_y2, I_FWD: to_core, T_Z: to_z, T_Y: to_y6, T_FWD: to_z}
    part = rows // CHUNKS

    load_i = pltpu.make_async_copy(image_ref, images.at[pl.ds(0, rows)], local_sem.at[0])
    load_t = pltpu.make_async_copy(text_ref, texts.at[pl.ds(0, rows)], local_sem.at[1])
    load_i.start()
    load_t.start()
    barrier = pltpu.get_barrier_semaphore()
    for other in (to_y2, to_y6, to_core, to_z):
        pl.semaphore_signal(barrier, inc=1, device_id=other, device_id_type=MESH)
    pl.semaphore_wait(barrier, 4)
    load_i.wait()
    load_t.wait()

    def gather(stream, k):
        held = images if stream < T_Z else texts
        source = {I_CORE: 0, I_Y: 0, I_FWD: 2, T_Z: 0, T_Y: 0, T_FWD: 2}[stream]
        target = {I_CORE: 1, I_Y: 2, I_FWD: 3, T_Z: 1, T_Y: 2, T_FWD: 3}[stream]
        return pltpu.make_async_remote_copy(
            src_ref=held.at[pl.ds(source * rows + k * part, part)],
            dst_ref=held.at[pl.ds(target * rows + k * part, part)],
            send_sem=send_sem.at[stream, k],
            recv_sem=recv_sem.at[stream, k],
            device_id=partner[stream],
            device_id_type=MESH,
        )

    def back(stream, k):
        return pltpu.make_async_remote_copy(
            src_ref=staged.at[stream, pl.ds(k * part, part)],
            dst_ref=landed.at[stream, pl.ds(k * part, part)],
            send_sem=back_send.at[stream, k],
            recv_sem=back_recv.at[stream, k],
            device_id=partner[stream],
            device_id_type=MESH,
        )

    scale = scale_ref[0]
    bias = bias_ref[0]

    def fill_weights(i0, i1, t0, t1):
        block = lax.dot_general(
            images[pl.ds(i0 * rows, (i1 - i0) * rows)],
            texts[pl.ds(t0 * rows, (t1 - t0) * rows)],
            (((1,), (1,)), ((), ())),
            preferred_element_type=F32,
        )
        block = sigmoid(scale * block + bias)
        if i0 == 0 and t0 == 0:
            r = lax.broadcasted_iota(jnp.int32, block.shape, 0)
            c = lax.broadcasted_iota(jnp.int32, block.shape, 1)
            block = block - jnp.where((r == c) & (r < rows), 1.0, 0.0)
        weights[pl.ds(i0 * rows, (i1 - i0) * rows), pl.ds(t0 * rows, (t1 - t0) * rows)] = block.astype(BF16)

    def image_grad(i):
        return scale * jnp.dot(weights[pl.ds(i * rows, rows), :], texts[...], preferred_element_type=F32)

    def text_grad(t):
        return scale * lax.dot_general(
            weights[:, pl.ds(t * rows, rows)], images[...], (((0,), (0,)), ((), ())), preferred_element_type=F32
        )

    for k in range(CHUNKS):
        gather(I_Y, k).start()
        gather(T_Y, k).start()
        gather(T_Z, k).start()
        gather(I_CORE, k).start()
    for k in range(CHUNKS):
        gather(I_Y, k).wait_recv()
        gather(I_FWD, k).start()
        gather(T_Y, k).wait_recv()
        gather(T_FWD, k).start()
        if k == CHUNKS - 2:
            for j in range(CHUNKS):
                gather(I_CORE, j).wait_recv()
                gather(T_Z, j).wait_recv()
            fill_weights(0, 2, 0, 2)
    for k in range(CHUNKS):
        gather(I_FWD, k).wait_recv()
    fill_weights(2, 4, 0, 2)
    for k in range(CHUNKS):
        gather(T_FWD, k).wait_recv()
    fill_weights(0, 4, 2, 4)

    staged[T_FWD] = text_grad(3).astype(BF16)
    for k in range(CHUNKS):
        back(T_FWD, k).start()
    staged[I_FWD] = image_grad(3).astype(BF16)
    for k in range(CHUNKS):
        back(I_FWD, k).start()
    image_acc[...] = image_grad(2)
    for k in range(CHUNKS):
        back(I_FWD, k).wait_recv()
        at = pl.ds(k * part, part)
        staged[I_Y, at] = (image_acc[at] + landed[I_FWD, at].astype(F32)).astype(BF16)
        back(I_Y, k).start()
    text_acc[...] = text_grad(2)
    staged[T_Z] = text_grad(1).astype(BF16)
    for k in range(CHUNKS):
        back(T_FWD, k).wait_recv()
        at = pl.ds(k * part, part)
        staged[T_Y, at] = (text_acc[at] + landed[T_FWD, at].astype(F32)).astype(BF16)
        back(T_Y, k).start()
        back(T_Z, k).start()
    staged[I_CORE] = image_grad(1).astype(BF16)
    for k in range(CHUNKS):
        back(I_CORE, k).start()
    image_acc[...] = image_grad(0)
    text_acc[...] = text_grad(0)
    for k in range(CHUNKS):
        at = pl.ds(k * part, part)
        back(I_CORE, k).wait_recv()
        back(T_Z, k).wait_recv()
        image_acc[at] = image_acc[at] + landed[I_CORE, at].astype(F32)
        text_acc[at] = text_acc[at] + landed[T_Z, at].astype(F32)
    for k in range(CHUNKS):
        at = pl.ds(k * part, part)
        back(I_Y, k).wait_recv()
        grad_image_ref[at] = (image_acc[at] + landed[I_Y, at].astype(F32)).astype(BF16)
        back(T_Y, k).wait_recv()
        grad_text_ref[at] = (text_acc[at] + landed[T_Y, at].astype(F32)).astype(BF16)
    for stream in range(6):
        for k in range(CHUNKS):
            gather(stream, k).wait_send()
            back(stream, k).wait_send()

def write_out(image_ref, text_ref, grad_image_ref, grad_text_ref, sem):
    copies = [
        pltpu.make_async_copy(image_ref, grad_image_ref, sem.at[0]),
        pltpu.make_async_copy(text_ref, grad_text_ref, sem.at[1]),
    ]
    for copy in copies:
        copy.start()
    for copy in copies:
        copy.wait()


def per_device(image_rows, text_rows, logit_scale, logit_bias):
    rows, width = image_rows.shape
    quarter = lax.axis_size("dp") // 4
    shape = jax.ShapeDtypeStruct((rows, width), BF16)
    vmem = pl.BlockSpec(memory_space=pltpu.VMEM)
    hbm = pl.BlockSpec(memory_space=pltpu.HBM)
    smem = pl.BlockSpec(memory_space=pltpu.SMEM)
    dma = pltpu.SemaphoreType.DMA
    sums = pl.pallas_call(
        functools.partial(kernel, quarter, rows),
        out_shape=(pltpu.VMEM((rows, width), BF16), pltpu.VMEM((rows, width), BF16)),
        in_specs=[smem, smem, hbm, hbm],
        out_specs=(vmem, vmem),
        scratch_shapes=[
            pltpu.VMEM((4 * rows, width), BF16),
            pltpu.VMEM((4 * rows, width), BF16),
            pltpu.VMEM((4 * rows, 4 * rows), BF16),
            pltpu.VMEM((rows, width), F32),
            pltpu.VMEM((rows, width), F32),
            pltpu.VMEM((6, rows, width), BF16),
            pltpu.VMEM((6, rows, width), BF16),
            dma((6, CHUNKS)),
            dma((6, CHUNKS)),
            dma((6, CHUNKS)),
            dma((6, CHUNKS)),
            dma((2,)),
        ],
        compiler_params=pltpu.CompilerParams(
            collective_id=0, has_side_effects=True, vmem_limit_bytes=48 * 1024 * 1024
        ),
        cost_estimate=pl.CostEstimate(
            flops=6 * rows * rows * 16 * width, bytes_accessed=8 * rows * width, transcendentals=16 * rows * rows
        ),
        name="contrastive",
    )(logit_scale, logit_bias, *(pltpu.with_memory_space_constraint(a, pltpu.HBM) for a in (image_rows, text_rows)))
    return pl.pallas_call(
        write_out,
        out_shape=(shape, shape),
        in_specs=[vmem, vmem],
        out_specs=(hbm, hbm),
        scratch_shapes=[dma((2,))],
        compiler_params=pltpu.CompilerParams(vmem_limit_bytes=4 * 1024 * 1024),
        name="write_out",
    )(*sums)


def solution(mesh):
    split = P(("dp", "rows"), None)
    return jax.shard_map(
        per_device,
        mesh=mesh,
        in_specs=(split, split, P(), P()),
        out_specs=(split, split),
        check_vma=False,
    )
```

```python
import functools

import jax
import jax.numpy as jnp
from jax import lax
from jax.experimental import pallas as pl
from jax.experimental.pallas import tpu as pltpu
from jax.sharding import PartitionSpec as P

MESH = pl.DeviceIdType.MESH
CHUNKS = 4
LEAD = 4
F32 = jnp.float32
BF16 = jnp.bfloat16

I_CORE, I_Y, I_FWD, T_Z, T_Y, T_FWD = range(6)


def sigmoid(x):
    return 1.0 / (1.0 + jnp.exp(-x))


def kernel(
    quarter, rows, scale_ref, bias_ref, image_ref, text_ref, grad_image_ref, grad_text_ref,
    images, texts, weights, image_acc, text_acc, staged, landed,
    send_sem, recv_sem, back_send, back_recv, local_sem,
):
    dp, row = lax.axis_index("dp"), lax.axis_index("rows")
    low = quarter - 2 * quarter * ((dp // quarter) % 2)
    high = 2 * quarter - 4 * quarter * ((dp // (2 * quarter)) % 2)
    to_y2 = {"dp": dp + low, "rows": row}
    to_y6 = {"dp": dp + low + high, "rows": row}
    to_core = {"dp": dp, "rows": row + 1 - 2 * (row % 2)}
    to_z = {"dp": dp, "rows": row + 2 - 4 * (row // 2)}
    partner = {I_CORE: to_core, I_Y: to_y2, I_FWD: to_core, T_Z: to_z, T_Y: to_y6, T_FWD: to_z}
    part = rows // CHUNKS

    load_i = pltpu.make_async_copy(image_ref, images.at[pl.ds(0, rows)], local_sem.at[0])
    load_t = pltpu.make_async_copy(text_ref, texts.at[pl.ds(0, rows)], local_sem.at[1])
    load_i.start()
    load_t.start()
    barrier = pltpu.get_barrier_semaphore()
    for other in (to_y2, to_y6, to_core, to_z):
        pl.semaphore_signal(barrier, inc=1, device_id=other, device_id_type=MESH)
    pl.semaphore_wait(barrier, 4)
    load_i.wait()
    load_t.wait()

    def gather(stream, k):
        held = images if stream < T_Z else texts
        source = {I_CORE: 0, I_Y: 0, I_FWD: 2, T_Z: 0, T_Y: 0, T_FWD: 2}[stream]
        target = {I_CORE: 1, I_Y: 2, I_FWD: 3, T_Z: 1, T_Y: 2, T_FWD: 3}[stream]
        return pltpu.make_async_remote_copy(
            src_ref=held.at[pl.ds(source * rows + k * part, part)],
            dst_ref=held.at[pl.ds(target * rows + k * part, part)],
            send_sem=send_sem.at[stream, k],
            recv_sem=recv_sem.at[stream, k],
            device_id=partner[stream],
            device_id_type=MESH,
        )

    def back(stream, k):
        return pltpu.make_async_remote_copy(
            src_ref=staged.at[stream, pl.ds(k * part, part)],
            dst_ref=landed.at[stream, pl.ds(k * part, part)],
            send_sem=back_send.at[stream, k],
            recv_sem=back_recv.at[stream, k],
            device_id=partner[stream],
            device_id_type=MESH,
        )

    scale = scale_ref[0]
    bias = bias_ref[0]

    def fill_weights(i0, i1, t0, t1):
        block = lax.dot_general(
            images[pl.ds(i0 * rows, (i1 - i0) * rows)],
            texts[pl.ds(t0 * rows, (t1 - t0) * rows)],
            (((1,), (1,)), ((), ())),
            preferred_element_type=F32,
        )
        block = sigmoid(scale * block + bias)
        if i0 == 0 and t0 == 0:
            r = lax.broadcasted_iota(jnp.int32, block.shape, 0)
            c = lax.broadcasted_iota(jnp.int32, block.shape, 1)
            block = block - jnp.where((r == c) & (r < rows), 1.0, 0.0)
        weights[pl.ds(i0 * rows, (i1 - i0) * rows), pl.ds(t0 * rows, (t1 - t0) * rows)] = block.astype(BF16)

    def image_grad(i):
        return scale * jnp.dot(weights[pl.ds(i * rows, rows), :], texts[...], preferred_element_type=F32)

    def text_grad(t):
        return scale * lax.dot_general(
            weights[:, pl.ds(t * rows, rows)], images[...], (((0,), (0,)), ((), ())), preferred_element_type=F32
        )

    odd = (dp // (quarter // 2)) % 2

    @pl.when(odd == 0)
    def _():
        for k in range(CHUNKS):
            gather(I_Y, k).start()
            gather(T_Y, k).start()

    for k in range(CHUNKS):
        gather(T_Z, k).start()
        gather(I_CORE, k).start()

    @pl.when(odd == 1)
    def _():
        for k in range(LEAD):
            gather(T_Z, k).wait_recv()
        for k in range(CHUNKS):
            gather(I_Y, k).start()
            gather(T_Y, k).start()
    for k in range(CHUNKS):
        gather(I_Y, k).wait_recv()
        gather(I_FWD, k).start()
        gather(T_Y, k).wait_recv()
        gather(T_FWD, k).start()
        if k == CHUNKS - 2:
            for j in range(CHUNKS):
                gather(I_CORE, j).wait_recv()
                if j >= LEAD:
                    gather(T_Z, j).wait_recv()

            @pl.when(odd == 0)
            def _():
                for j in range(LEAD):
                    gather(T_Z, j).wait_recv()

            fill_weights(0, 2, 0, 2)
    for k in range(CHUNKS):
        gather(I_FWD, k).wait_recv()
    fill_weights(2, 4, 0, 2)
    for k in range(CHUNKS):
        gather(T_FWD, k).wait_recv()
    fill_weights(0, 4, 2, 4)

    staged[T_FWD] = text_grad(3).astype(BF16)
    for k in range(CHUNKS):
        back(T_FWD, k).start()
    staged[I_FWD] = image_grad(3).astype(BF16)
    for k in range(CHUNKS):
        back(I_FWD, k).start()
    image_acc[...] = image_grad(2)
    for k in range(CHUNKS):
        back(I_FWD, k).wait_recv()
        at = pl.ds(k * part, part)
        staged[I_Y, at] = (image_acc[at] + landed[I_FWD, at].astype(F32)).astype(BF16)
        back(I_Y, k).start()
    text_acc[...] = text_grad(2)
    staged[T_Z] = text_grad(1).astype(BF16)
    for k in range(CHUNKS):
        back(T_FWD, k).wait_recv()
        at = pl.ds(k * part, part)
        staged[T_Y, at] = (text_acc[at] + landed[T_FWD, at].astype(F32)).astype(BF16)
        back(T_Y, k).start()
        back(T_Z, k).start()
    staged[I_CORE] = image_grad(1).astype(BF16)
    for k in range(CHUNKS):
        back(I_CORE, k).start()
    image_acc[...] = image_grad(0)
    text_acc[...] = text_grad(0)
    for k in range(CHUNKS):
        at = pl.ds(k * part, part)
        back(I_CORE, k).wait_recv()
        back(T_Z, k).wait_recv()
        image_acc[at] = image_acc[at] + landed[I_CORE, at].astype(F32)
        text_acc[at] = text_acc[at] + landed[T_Z, at].astype(F32)
    for k in range(CHUNKS):
        at = pl.ds(k * part, part)
        back(I_Y, k).wait_recv()
        grad_image_ref[at] = (image_acc[at] + landed[I_Y, at].astype(F32)).astype(BF16)
        back(T_Y, k).wait_recv()
        grad_text_ref[at] = (text_acc[at] + landed[T_Y, at].astype(F32)).astype(BF16)
    for stream in range(6):
        for k in range(CHUNKS):
            gather(stream, k).wait_send()
            back(stream, k).wait_send()

def write_out(image_ref, text_ref, grad_image_ref, grad_text_ref, sem):
    copies = [
        pltpu.make_async_copy(image_ref, grad_image_ref, sem.at[0]),
        pltpu.make_async_copy(text_ref, grad_text_ref, sem.at[1]),
    ]
    for copy in copies:
        copy.start()
    for copy in copies:
        copy.wait()


def per_device(image_rows, text_rows, logit_scale, logit_bias):
    rows, width = image_rows.shape
    quarter = lax.axis_size("dp") // 4
    shape = jax.ShapeDtypeStruct((rows, width), BF16)
    vmem = pl.BlockSpec(memory_space=pltpu.VMEM)
    hbm = pl.BlockSpec(memory_space=pltpu.HBM)
    smem = pl.BlockSpec(memory_space=pltpu.SMEM)
    dma = pltpu.SemaphoreType.DMA
    sums = pl.pallas_call(
        functools.partial(kernel, quarter, rows),
        out_shape=(pltpu.VMEM((rows, width), BF16), pltpu.VMEM((rows, width), BF16)),
        in_specs=[smem, smem, hbm, hbm],
        out_specs=(vmem, vmem),
        scratch_shapes=[
            pltpu.VMEM((4 * rows, width), BF16),
            pltpu.VMEM((4 * rows, width), BF16),
            pltpu.VMEM((4 * rows, 4 * rows), BF16),
            pltpu.VMEM((rows, width), F32),
            pltpu.VMEM((rows, width), F32),
            pltpu.VMEM((6, rows, width), BF16),
            pltpu.VMEM((6, rows, width), BF16),
            dma((6, CHUNKS)),
            dma((6, CHUNKS)),
            dma((6, CHUNKS)),
            dma((6, CHUNKS)),
            dma((2,)),
        ],
        compiler_params=pltpu.CompilerParams(
            collective_id=0, has_side_effects=True, vmem_limit_bytes=48 * 1024 * 1024
        ),
        cost_estimate=pl.CostEstimate(
            flops=6 * rows * rows * 16 * width, bytes_accessed=8 * rows * width, transcendentals=16 * rows * rows
        ),
        name="contrastive",
    )(logit_scale, logit_bias, *(pltpu.with_memory_space_constraint(a, pltpu.HBM) for a in (image_rows, text_rows)))
    return pl.pallas_call(
        write_out,
        out_shape=(shape, shape),
        in_specs=[vmem, vmem],
        out_specs=(hbm, hbm),
        scratch_shapes=[dma((2,))],
        compiler_params=pltpu.CompilerParams(vmem_limit_bytes=4 * 1024 * 1024),
        name="write_out",
    )(*sums)


def solution(mesh):
    split = P(("dp", "rows"), None)
    return jax.shard_map(
        per_device,
        mesh=mesh,
        in_specs=(split, split, P(), P()),
        out_specs=(split, split),
        check_vma=False,
    )
```

```python
import functools

import jax
import jax.numpy as jnp
from jax import lax
from jax.experimental import pallas as pl
from jax.experimental.pallas import tpu as pltpu
from jax.sharding import PartitionSpec as P

MESH = pl.DeviceIdType.MESH
CHUNKS = 4
LEAD = 4
EARLY = 2
AHEAD = 2
F32 = jnp.float32
BF16 = jnp.bfloat16

I_CORE, I_Y, I_FWD, T_Z, T_Y, T_FWD = range(6)


def sigmoid(x):
    return 1.0 / (1.0 + jnp.exp(-x))


def kernel(
    quarter, rows, scale_ref, bias_ref, image_ref, text_ref, grad_image_ref, grad_text_ref,
    images, texts, near, far, image_acc, text_acc, staged, landed,
    send_sem, recv_sem, back_send, back_recv, local_sem,
):
    dp, row = lax.axis_index("dp"), lax.axis_index("rows")
    low = quarter - 2 * quarter * ((dp // quarter) % 2)
    high = 2 * quarter - 4 * quarter * ((dp // (2 * quarter)) % 2)
    to_y2 = {"dp": dp + low, "rows": row}
    to_y6 = {"dp": dp + low + high, "rows": row}
    to_core = {"dp": dp, "rows": row + 1 - 2 * (row % 2)}
    to_z = {"dp": dp, "rows": row + 2 - 4 * (row // 2)}
    partner = {I_CORE: to_core, I_Y: to_y2, I_FWD: to_core, T_Z: to_z, T_Y: to_y6, T_FWD: to_z}
    part = rows // CHUNKS

    load_i = pltpu.make_async_copy(image_ref, images.at[pl.ds(0, rows)], local_sem.at[0])
    load_t = pltpu.make_async_copy(text_ref, texts.at[pl.ds(0, rows)], local_sem.at[1])
    load_i.start()
    load_t.start()
    barrier = pltpu.get_barrier_semaphore()
    for other in (to_y2, to_y6, to_core, to_z):
        pl.semaphore_signal(barrier, inc=1, device_id=other, device_id_type=MESH)
    pl.semaphore_wait(barrier, 4)
    load_i.wait()
    load_t.wait()

    def gather(stream, k):
        held = images if stream < T_Z else texts
        source = {I_CORE: 0, I_Y: 0, I_FWD: 2, T_Z: 0, T_Y: 0, T_FWD: 2}[stream]
        target = {I_CORE: 1, I_Y: 2, I_FWD: 3, T_Z: 1, T_Y: 2, T_FWD: 3}[stream]
        return pltpu.make_async_remote_copy(
            src_ref=held.at[pl.ds(source * rows + k * part, part)],
            dst_ref=held.at[pl.ds(target * rows + k * part, part)],
            send_sem=send_sem.at[stream, k],
            recv_sem=recv_sem.at[stream, k],
            device_id=partner[stream],
            device_id_type=MESH,
        )

    def back(stream, k):
        return pltpu.make_async_remote_copy(
            src_ref=staged.at[stream, pl.ds(k * part, part)],
            dst_ref=landed.at[stream, pl.ds(k * part, part)],
            send_sem=back_send.at[stream, k],
            recv_sem=back_recv.at[stream, k],
            device_id=partner[stream],
            device_id_type=MESH,
        )

    scale = scale_ref[0]
    bias = bias_ref[0]

    def fill_near(i0, i1):
        block = lax.dot_general(
            images[pl.ds(i0 * rows, (i1 - i0) * rows)], texts[pl.ds(0, 2 * rows)], (((1,), (1,)), ((), ())), preferred_element_type=F32
        )
        block = sigmoid(scale * block + bias)
        if i0 == 0:
            r = lax.broadcasted_iota(jnp.int32, block.shape, 0)
            c = lax.broadcasted_iota(jnp.int32, block.shape, 1)
            block = block - jnp.where((r == c) & (r < rows), 1.0, 0.0)
        near[pl.ds(i0 * rows, (i1 - i0) * rows)] = block.astype(BF16)

    def fill_far(start, size):
        block = lax.dot_general(
            texts[pl.ds(2 * rows + start, size)], images[...], (((1,), (1,)), ((), ())), preferred_element_type=F32
        )
        far[pl.ds(start, size)] = sigmoid(scale * block + bias).astype(BF16)

    def near_images(i, n):
        return jnp.dot(near[pl.ds(i * rows, n * rows)], texts[pl.ds(0, 2 * rows)], preferred_element_type=F32)

    def far_images(i, n, start, size):
        return lax.dot_general(
            far[pl.ds(start, size), pl.ds(i * rows, n * rows)],
            texts[pl.ds(2 * rows + start, size)],
            (((0,), (0,)), ((), ())),
            preferred_element_type=F32,
        )

    def near_texts(t):
        return scale * lax.dot_general(
            near[:, pl.ds(t * rows, rows)], images[...], (((0,), (0,)), ((), ())), preferred_element_type=F32
        )

    def far_texts(start, size):
        return scale * jnp.dot(far[pl.ds(start, size)], images[...], preferred_element_type=F32)

    odd = (dp // (quarter // 2)) % 2

    @pl.when(odd == 0)
    def _():
        for k in range(CHUNKS):
            gather(I_Y, k).start()
            gather(T_Y, k).start()

    for k in range(CHUNKS):
        gather(T_Z, k).start()
        gather(I_CORE, k).start()

    @pl.when(odd == 1)
    def _():
        for k in range(LEAD):
            gather(T_Z, k).wait_recv()
        for k in range(CHUNKS):
            gather(I_Y, k).start()
            gather(T_Y, k).start()
    for k in range(CHUNKS):
        gather(I_Y, k).wait_recv()
        gather(I_FWD, k).start()
        gather(T_Y, k).wait_recv()
        gather(T_FWD, k).start()
        if k == CHUNKS - 2:
            for j in range(CHUNKS):
                gather(I_CORE, j).wait_recv()
                if j >= LEAD:
                    gather(T_Z, j).wait_recv()

            @pl.when(odd == 0)
            def _():
                for j in range(LEAD):
                    gather(T_Z, j).wait_recv()

            fill_near(0, 2)
    for k in range(CHUNKS):
        gather(I_FWD, k).wait_recv()
    fill_near(2, 4)
    staged[T_Z] = near_texts(1).astype(BF16)

    @pl.when(odd == 1)
    def _():
        for k in range(EARLY):
            back(T_Z, k).start()

    head = rows - part
    for k in range(CHUNKS - 1):
        gather(T_FWD, k).wait_recv()
    fill_far(rows, head)
    staged[T_FWD, pl.ds(0, head)] = far_texts(rows, head).astype(BF16)

    for k in range(CHUNKS - 1):
        back(T_FWD, k).start()

    fill_far(0, rows)
    image_acc[...] = near_images(2, 2) + far_images(2, 2, 0, rows + head)
    text_acc[...] = far_texts(0, rows)
    gather(T_FWD, CHUNKS - 1).wait_recv()

    fill_far(rows + head, part)
    staged[T_FWD, pl.ds(head, part)] = far_texts(rows + head, part).astype(BF16)
    back(T_FWD, CHUNKS - 1).start()
    image_acc[...] = scale * (image_acc[...] + far_images(2, 2, rows + head, part))
    staged[I_FWD] = image_acc[pl.ds(rows, rows)].astype(BF16)
    for k in range(CHUNKS):
        back(I_FWD, k).start()
    for k in range(CHUNKS):
        back(I_FWD, k).wait_recv()
        at = pl.ds(k * part, part)
        staged[I_Y, at] = (image_acc[at] + landed[I_FWD, at].astype(F32)).astype(BF16)
        back(I_Y, k).start()
    for k in range(CHUNKS):
        back(T_FWD, k).wait_recv()
        at = pl.ds(k * part, part)
        staged[T_Y, at] = (text_acc[at] + landed[T_FWD, at].astype(F32)).astype(BF16)
        back(T_Y, k).start()
        if k == CHUNKS - 1 - AHEAD:

            @pl.when(odd == 0)
            def _():
                for j in range(CHUNKS):
                    back(T_Z, j).start()

            @pl.when(odd == 1)
            def _():
                for j in range(EARLY, CHUNKS):
                    back(T_Z, j).start()

    staged[I_CORE] = (scale * (near_images(1, 1) + far_images(1, 1, 0, 2 * rows))).astype(BF16)
    for k in range(CHUNKS):
        back(I_CORE, k).start()
    image_acc[pl.ds(0, rows)] = scale * (near_images(0, 1) + far_images(0, 1, 0, 2 * rows))
    text_acc[...] = near_texts(0)
    for k in range(CHUNKS):
        at = pl.ds(k * part, part)
        back(I_CORE, k).wait_recv()
        image_acc[at] = image_acc[at] + landed[I_CORE, at].astype(F32)
    for k in range(CHUNKS):
        for stream in range(6):
            gather(stream, k).wait_send()
        for stream in (I_CORE, I_FWD, T_FWD):
            back(stream, k).wait_send()
    for k in range(CHUNKS):
        at = pl.ds(k * part, part)
        if k == CHUNKS - 1:
            for j in range(CHUNKS):
                for stream in (I_Y, T_Z, T_Y):
                    back(stream, j).wait_send()
        back(I_Y, k).wait_recv()
        grad_image_ref[at] = (image_acc[at] + landed[I_Y, at].astype(F32)).astype(BF16)
        back(T_Z, k).wait_recv()
        back(T_Y, k).wait_recv()
        grad_text_ref[at] = (text_acc[at] + landed[T_Z, at].astype(F32) + landed[T_Y, at].astype(F32)).astype(BF16)

def write_out(image_ref, text_ref, grad_image_ref, grad_text_ref, sem):
    copies = [
        pltpu.make_async_copy(image_ref, grad_image_ref, sem.at[0]),
        pltpu.make_async_copy(text_ref, grad_text_ref, sem.at[1]),
    ]
    for copy in copies:
        copy.start()
    for copy in copies:
        copy.wait()


def per_device(image_rows, text_rows, logit_scale, logit_bias):
    rows, width = image_rows.shape
    quarter = lax.axis_size("dp") // 4
    shape = jax.ShapeDtypeStruct((rows, width), BF16)
    vmem = pl.BlockSpec(memory_space=pltpu.VMEM)
    hbm = pl.BlockSpec(memory_space=pltpu.HBM)
    smem = pl.BlockSpec(memory_space=pltpu.SMEM)
    dma = pltpu.SemaphoreType.DMA
    sums = pl.pallas_call(
        functools.partial(kernel, quarter, rows),
        out_shape=(pltpu.VMEM((rows, width), BF16), pltpu.VMEM((rows, width), BF16)),
        in_specs=[smem, smem, hbm, hbm],
        out_specs=(vmem, vmem),
        scratch_shapes=[
            pltpu.VMEM((4 * rows, width), BF16),
            pltpu.VMEM((4 * rows, width), BF16),
            pltpu.VMEM((4 * rows, 2 * rows), BF16),
            pltpu.VMEM((2 * rows, 4 * rows), BF16),
            pltpu.VMEM((2 * rows, width), F32),
            pltpu.VMEM((rows, width), F32),
            pltpu.VMEM((6, rows, width), BF16),
            pltpu.VMEM((6, rows, width), BF16),
            dma((6, CHUNKS)),
            dma((6, CHUNKS)),
            dma((6, CHUNKS)),
            dma((6, CHUNKS)),
            dma((2,)),
        ],
        compiler_params=pltpu.CompilerParams(
            collective_id=0, has_side_effects=True, vmem_limit_bytes=48 * 1024 * 1024
        ),
        cost_estimate=pl.CostEstimate(
            flops=6 * rows * rows * 16 * width, bytes_accessed=8 * rows * width, transcendentals=16 * rows * rows
        ),
        name="contrastive",
    )(logit_scale, logit_bias, *(pltpu.with_memory_space_constraint(a, pltpu.HBM) for a in (image_rows, text_rows)))
    return pl.pallas_call(
        write_out,
        out_shape=(shape, shape),
        in_specs=[vmem, vmem],
        out_specs=(hbm, hbm),
        scratch_shapes=[dma((2,))],
        compiler_params=pltpu.CompilerParams(vmem_limit_bytes=4 * 1024 * 1024),
        name="write_out",
    )(*sums)


def solution(mesh):
    split = P(("dp", "rows"), None)
    return jax.shard_map(
        per_device,
        mesh=mesh,
        in_specs=(split, split, P(), P()),
        out_specs=(split, split),
        check_vma=False,
    )
```

```python
import functools

import jax
import jax.numpy as jnp
from jax import lax
from jax.experimental import pallas as pl
from jax.experimental.pallas import tpu as pltpu
from jax.sharding import PartitionSpec as P

MESH = pl.DeviceIdType.MESH
CHUNKS = 4
LEAD = 4
EARLY = 1
ACROSS = 1
AHEAD = 2
F32 = jnp.float32
BF16 = jnp.bfloat16

I_CORE, I_Y, I_FWD, T_Z, T_Y, T_FWD = range(6)


def sigmoid(x):
    return 1.0 / (1.0 + jnp.exp(-x))


def kernel(
    quarter, rows, scale_ref, bias_ref, image_ref, text_ref, grad_image_ref, grad_text_ref,
    images, texts, near, far, image_acc, text_acc, staged, landed,
    send_sem, recv_sem, back_send, back_recv, local_sem,
):
    dp, row = lax.axis_index("dp"), lax.axis_index("rows")
    low = quarter - 2 * quarter * ((dp // quarter) % 2)
    high = 2 * quarter - 4 * quarter * ((dp // (2 * quarter)) % 2)
    to_y2 = {"dp": dp + low, "rows": row}
    to_y6 = {"dp": dp + low + high, "rows": row}
    to_core = {"dp": dp, "rows": row + 1 - 2 * (row % 2)}
    to_z = {"dp": dp, "rows": row + 2 - 4 * (row // 2)}
    partner = {I_CORE: to_core, I_Y: to_y2, I_FWD: to_core, T_Z: to_z, T_Y: to_y6, T_FWD: to_z}
    part = rows // CHUNKS

    load_i = pltpu.make_async_copy(image_ref, images.at[pl.ds(0, rows)], local_sem.at[0])
    load_t = pltpu.make_async_copy(text_ref, texts.at[pl.ds(0, rows)], local_sem.at[1])
    load_i.start()
    load_t.start()
    barrier = pltpu.get_barrier_semaphore()
    for other in (to_y2, to_y6, to_core, to_z):
        pl.semaphore_signal(barrier, inc=1, device_id=other, device_id_type=MESH)
    pl.semaphore_wait(barrier, 4)
    load_i.wait()
    load_t.wait()

    def gather(stream, k):
        held = images if stream < T_Z else texts
        source = {I_CORE: 0, I_Y: 0, I_FWD: 2, T_Z: 0, T_Y: 0, T_FWD: 2}[stream]
        target = {I_CORE: 1, I_Y: 2, I_FWD: 3, T_Z: 1, T_Y: 2, T_FWD: 3}[stream]
        return pltpu.make_async_remote_copy(
            src_ref=held.at[pl.ds(source * rows + k * part, part)],
            dst_ref=held.at[pl.ds(target * rows + k * part, part)],
            send_sem=send_sem.at[stream, k],
            recv_sem=recv_sem.at[stream, k],
            device_id=partner[stream],
            device_id_type=MESH,
        )

    def back(stream, k):
        return pltpu.make_async_remote_copy(
            src_ref=staged.at[stream, pl.ds(k * part, part)],
            dst_ref=landed.at[stream, pl.ds(k * part, part)],
            send_sem=back_send.at[stream, k],
            recv_sem=back_recv.at[stream, k],
            device_id=partner[stream],
            device_id_type=MESH,
        )

    def across(k):
        return pltpu.make_async_remote_copy(
            src_ref=texts.at[pl.ds(rows + k * part, part)],
            dst_ref=texts.at[pl.ds(3 * rows + k * part, part)],
            send_sem=send_sem.at[T_FWD, k],
            recv_sem=recv_sem.at[T_FWD, k],
            device_id=to_y6,
            device_id_type=MESH,
        )

    scale = scale_ref[0]
    bias = bias_ref[0]

    def fill_near(i0, i1):
        block = lax.dot_general(
            images[pl.ds(i0 * rows, (i1 - i0) * rows)], texts[pl.ds(0, 2 * rows)], (((1,), (1,)), ((), ())), preferred_element_type=F32
        )
        block = sigmoid(scale * block + bias)
        if i0 == 0:
            r = lax.broadcasted_iota(jnp.int32, block.shape, 0)
            c = lax.broadcasted_iota(jnp.int32, block.shape, 1)
            block = block - jnp.where((r == c) & (r < rows), 1.0, 0.0)
        near[pl.ds(i0 * rows, (i1 - i0) * rows)] = block.astype(BF16)

    def fill_far(start, size):
        block = lax.dot_general(
            texts[pl.ds(2 * rows + start, size)], images[...], (((1,), (1,)), ((), ())), preferred_element_type=F32
        )
        far[pl.ds(start, size)] = sigmoid(scale * block + bias).astype(BF16)

    def near_images(i, n):
        return jnp.dot(near[pl.ds(i * rows, n * rows)], texts[pl.ds(0, 2 * rows)], preferred_element_type=F32)

    def far_images(i, n, start, size):
        return lax.dot_general(
            far[pl.ds(start, size), pl.ds(i * rows, n * rows)],
            texts[pl.ds(2 * rows + start, size)],
            (((0,), (0,)), ((), ())),
            preferred_element_type=F32,
        )

    def near_texts(t):
        return scale * lax.dot_general(
            near[:, pl.ds(t * rows, rows)], images[...], (((0,), (0,)), ((), ())), preferred_element_type=F32
        )

    def far_texts(start, size):
        return scale * jnp.dot(far[pl.ds(start, size)], images[...], preferred_element_type=F32)

    odd = (dp // (quarter // 2)) % 2

    @pl.when(odd == 0)
    def _():
        for k in range(CHUNKS):
            gather(I_Y, k).start()
            gather(T_Y, k).start()

    for k in range(CHUNKS):
        gather(T_Z, k).start()
        gather(I_CORE, k).start()

    @pl.when(odd == 1)
    def _():
        for k in range(LEAD):
            gather(T_Z, k).wait_recv()
        for k in range(CHUNKS):
            gather(I_Y, k).start()
            gather(T_Y, k).start()
        for k in range(CHUNKS - ACROSS, CHUNKS):
            across(k).start()
    for k in range(CHUNKS):
        gather(I_Y, k).wait_recv()
        gather(I_FWD, k).start()
        gather(T_Y, k).wait_recv()
        if k < CHUNKS - ACROSS:
            gather(T_FWD, k).start()
        else:

            @pl.when(odd == 0)
            def _():
                gather(T_FWD, k).start()

        if k == CHUNKS - 2:
            for j in range(CHUNKS):
                gather(I_CORE, j).wait_recv()
                if j >= LEAD:
                    gather(T_Z, j).wait_recv()

            @pl.when(odd == 0)
            def _():
                for j in range(LEAD):
                    gather(T_Z, j).wait_recv()

            fill_near(0, 2)
    for k in range(CHUNKS):
        gather(I_FWD, k).wait_recv()
    fill_near(2, 4)
    staged[T_Z] = near_texts(1).astype(BF16)

    @pl.when(odd == 1)
    def _():
        for k in range(EARLY):
            back(T_Z, k).start()

    head = rows - part
    for k in range(CHUNKS - 1):
        gather(T_FWD, k).wait_recv()
    fill_far(rows, head)
    staged[T_FWD, pl.ds(0, head)] = far_texts(rows, head).astype(BF16)

    for k in range(CHUNKS - 1):
        back(T_FWD, k).start()

    fill_far(0, rows)
    image_acc[...] = near_images(2, 2) + far_images(2, 2, 0, rows + head)
    text_acc[...] = far_texts(0, rows)
    gather(T_FWD, CHUNKS - 1).wait_recv()

    fill_far(rows + head, part)
    staged[T_FWD, pl.ds(head, part)] = far_texts(rows + head, part).astype(BF16)
    back(T_FWD, CHUNKS - 1).start()
    image_acc[...] = scale * (image_acc[...] + far_images(2, 2, rows + head, part))
    staged[I_FWD] = image_acc[pl.ds(rows, rows)].astype(BF16)
    for k in range(CHUNKS):
        back(I_FWD, k).start()
    for k in range(CHUNKS):
        back(I_FWD, k).wait_recv()
        at = pl.ds(k * part, part)
        staged[I_Y, at] = (image_acc[at] + landed[I_FWD, at].astype(F32)).astype(BF16)
        back(I_Y, k).start()
    for k in range(CHUNKS):
        back(T_FWD, k).wait_recv()
        at = pl.ds(k * part, part)
        staged[T_Y, at] = (text_acc[at] + landed[T_FWD, at].astype(F32)).astype(BF16)
        back(T_Y, k).start()
        if k == CHUNKS - 1 - AHEAD:

            @pl.when(odd == 0)
            def _():
                for j in range(CHUNKS):
                    back(T_Z, j).start()

            @pl.when(odd == 1)
            def _():
                for j in range(EARLY, CHUNKS):
                    back(T_Z, j).start()

    staged[I_CORE] = (scale * (near_images(1, 1) + far_images(1, 1, 0, 2 * rows))).astype(BF16)
    for k in range(CHUNKS):
        back(I_CORE, k).start()
    image_acc[pl.ds(0, rows)] = scale * (near_images(0, 1) + far_images(0, 1, 0, 2 * rows))
    text_acc[...] = near_texts(0)
    for k in range(CHUNKS):
        at = pl.ds(k * part, part)
        back(I_CORE, k).wait_recv()
        image_acc[at] = image_acc[at] + landed[I_CORE, at].astype(F32)
    for k in range(CHUNKS):
        for stream in range(6):
            gather(stream, k).wait_send()
        for stream in (I_CORE, I_FWD, T_FWD):
            back(stream, k).wait_send()
    for k in range(CHUNKS):
        at = pl.ds(k * part, part)
        if k == CHUNKS - 1:
            for j in range(CHUNKS):
                for stream in (I_Y, T_Z, T_Y):
                    back(stream, j).wait_send()
        back(I_Y, k).wait_recv()
        grad_image_ref[at] = (image_acc[at] + landed[I_Y, at].astype(F32)).astype(BF16)
        back(T_Z, k).wait_recv()
        back(T_Y, k).wait_recv()
        grad_text_ref[at] = (text_acc[at] + landed[T_Z, at].astype(F32) + landed[T_Y, at].astype(F32)).astype(BF16)

def write_out(image_ref, text_ref, grad_image_ref, grad_text_ref, sem):
    copies = [
        pltpu.make_async_copy(image_ref, grad_image_ref, sem.at[0]),
        pltpu.make_async_copy(text_ref, grad_text_ref, sem.at[1]),
    ]
    for copy in copies:
        copy.start()
    for copy in copies:
        copy.wait()


def per_device(image_rows, text_rows, logit_scale, logit_bias):
    rows, width = image_rows.shape
    quarter = lax.axis_size("dp") // 4
    shape = jax.ShapeDtypeStruct((rows, width), BF16)
    vmem = pl.BlockSpec(memory_space=pltpu.VMEM)
    hbm = pl.BlockSpec(memory_space=pltpu.HBM)
    smem = pl.BlockSpec(memory_space=pltpu.SMEM)
    dma = pltpu.SemaphoreType.DMA
    sums = pl.pallas_call(
        functools.partial(kernel, quarter, rows),
        out_shape=(pltpu.VMEM((rows, width), BF16), pltpu.VMEM((rows, width), BF16)),
        in_specs=[smem, smem, hbm, hbm],
        out_specs=(vmem, vmem),
        scratch_shapes=[
            pltpu.VMEM((4 * rows, width), BF16),
            pltpu.VMEM((4 * rows, width), BF16),
            pltpu.VMEM((4 * rows, 2 * rows), BF16),
            pltpu.VMEM((2 * rows, 4 * rows), BF16),
            pltpu.VMEM((2 * rows, width), F32),
            pltpu.VMEM((rows, width), F32),
            pltpu.VMEM((6, rows, width), BF16),
            pltpu.VMEM((6, rows, width), BF16),
            dma((6, CHUNKS)),
            dma((6, CHUNKS)),
            dma((6, CHUNKS)),
            dma((6, CHUNKS)),
            dma((2,)),
        ],
        compiler_params=pltpu.CompilerParams(
            collective_id=0, has_side_effects=True, vmem_limit_bytes=48 * 1024 * 1024
        ),
        cost_estimate=pl.CostEstimate(
            flops=6 * rows * rows * 16 * width, bytes_accessed=8 * rows * width, transcendentals=16 * rows * rows
        ),
        name="contrastive",
    )(logit_scale, logit_bias, *(pltpu.with_memory_space_constraint(a, pltpu.HBM) for a in (image_rows, text_rows)))
    return pl.pallas_call(
        write_out,
        out_shape=(shape, shape),
        in_specs=[vmem, vmem],
        out_specs=(hbm, hbm),
        scratch_shapes=[dma((2,))],
        compiler_params=pltpu.CompilerParams(vmem_limit_bytes=4 * 1024 * 1024),
        name="write_out",
    )(*sums)


def solution(mesh):
    split = P(("dp", "rows"), None)
    return jax.shard_map(
        per_device,
        mesh=mesh,
        in_specs=(split, split, P(), P()),
        out_specs=(split, split),
        check_vma=False,
    )
```

```python
import functools

import jax
import jax.numpy as jnp
from jax import lax
from jax.experimental import pallas as pl
from jax.experimental.pallas import tpu as pltpu
from jax.sharding import PartitionSpec as P

MESH = pl.DeviceIdType.MESH
CHUNKS = 4
LEAD = 4
EARLY = 2
AHEAD = 2
F32 = jnp.float32
BF16 = jnp.bfloat16

I_CORE, I_Y, I_FWD, T_Z, T_Y, T_FWD = range(6)


def sigmoid(x):
    return 1.0 / (1.0 + jnp.exp(-x))


def kernel(
    quarter, rows, scale_ref, bias_ref, image_ref, text_ref, grad_image_ref, grad_text_ref,
    images, texts, near, far, image_acc, text_acc, staged, landed,
    send_sem, recv_sem, back_send, back_recv, local_sem,
):
    dp, row = lax.axis_index("dp"), lax.axis_index("rows")
    low = quarter - 2 * quarter * ((dp // quarter) % 2)
    high = 2 * quarter - 4 * quarter * ((dp // (2 * quarter)) % 2)
    to_y2 = {"dp": dp + low, "rows": row}
    to_y6 = {"dp": dp + low + high, "rows": row}
    to_core = {"dp": dp, "rows": row + 1 - 2 * (row % 2)}
    to_z = {"dp": dp, "rows": row + 2 - 4 * (row // 2)}
    partner = {I_CORE: to_core, I_Y: to_y2, I_FWD: to_core, T_Z: to_z, T_Y: to_y6, T_FWD: to_z}
    part = rows // CHUNKS

    load_i = pltpu.make_async_copy(image_ref, images.at[pl.ds(0, rows)], local_sem.at[0])
    load_t = pltpu.make_async_copy(text_ref, texts.at[pl.ds(0, rows)], local_sem.at[1])
    load_i.start()
    load_t.start()
    barrier = pltpu.get_barrier_semaphore()
    for other in (to_y2, to_y6, to_core, to_z):
        pl.semaphore_signal(barrier, inc=1, device_id=other, device_id_type=MESH)
    pl.semaphore_wait(barrier, 4)
    load_i.wait()
    load_t.wait()

    def gather(stream, k):
        held = images if stream < T_Z else texts
        source = {I_CORE: 0, I_Y: 0, I_FWD: 2, T_Z: 0, T_Y: 0, T_FWD: 2}[stream]
        target = {I_CORE: 1, I_Y: 2, I_FWD: 3, T_Z: 1, T_Y: 2, T_FWD: 3}[stream]
        return pltpu.make_async_remote_copy(
            src_ref=held.at[pl.ds(source * rows + k * part, part)],
            dst_ref=held.at[pl.ds(target * rows + k * part, part)],
            send_sem=send_sem.at[stream, k],
            recv_sem=recv_sem.at[stream, k],
            device_id=partner[stream],
            device_id_type=MESH,
        )

    def back(stream, k):
        return pltpu.make_async_remote_copy(
            src_ref=staged.at[stream, pl.ds(k * part, part)],
            dst_ref=landed.at[stream, pl.ds(k * part, part)],
            send_sem=back_send.at[stream, k],
            recv_sem=back_recv.at[stream, k],
            device_id=partner[stream],
            device_id_type=MESH,
        )

    scale = scale_ref[0]
    bias = bias_ref[0]

    def fill_near(i0, i1):
        block = lax.dot_general(
            images[pl.ds(i0 * rows, (i1 - i0) * rows)], texts[pl.ds(0, 2 * rows)], (((1,), (1,)), ((), ())), preferred_element_type=F32
        )
        block = sigmoid(scale * block + bias)
        if i0 == 0:
            r = lax.broadcasted_iota(jnp.int32, block.shape, 0)
            c = lax.broadcasted_iota(jnp.int32, block.shape, 1)
            block = block - jnp.where((r == c) & (r < rows), 1.0, 0.0)
        near[pl.ds(i0 * rows, (i1 - i0) * rows)] = block.astype(BF16)

    def fill_far(start, size):
        block = lax.dot_general(
            texts[pl.ds(2 * rows + start, size)], images[...], (((1,), (1,)), ((), ())), preferred_element_type=F32
        )
        far[pl.ds(start, size)] = sigmoid(scale * block + bias).astype(BF16)

    def near_images(i, n):
        return jnp.dot(near[pl.ds(i * rows, n * rows)], texts[pl.ds(0, 2 * rows)], preferred_element_type=F32)

    def far_images(i, n, start, size):
        return lax.dot_general(
            far[pl.ds(start, size), pl.ds(i * rows, n * rows)],
            texts[pl.ds(2 * rows + start, size)],
            (((0,), (0,)), ((), ())),
            preferred_element_type=F32,
        )

    def near_texts(t):
        return scale * lax.dot_general(
            near[:, pl.ds(t * rows, rows)], images[...], (((0,), (0,)), ((), ())), preferred_element_type=F32
        )

    def far_texts(start, size):
        return scale * jnp.dot(far[pl.ds(start, size)], images[...], preferred_element_type=F32)

    odd = (dp // (quarter // 2)) % 2

    @pl.when(odd == 0)
    def _():
        for k in range(CHUNKS):
            gather(T_Y, k).start()
            gather(I_Y, k).start()

    for k in range(CHUNKS):
        gather(T_Z, k).start()
        gather(I_CORE, k).start()

    @pl.when(odd == 1)
    def _():
        for k in range(LEAD):
            gather(T_Z, k).wait_recv()
        for k in range(CHUNKS):
            gather(T_Y, k).start()
            gather(I_Y, k).start()
    for k in range(CHUNKS):
        gather(T_Y, k).wait_recv()
        gather(T_FWD, k).start()
        gather(I_Y, k).wait_recv()
        gather(I_FWD, k).start()
        if k == CHUNKS - 2:
            for j in range(CHUNKS):
                gather(I_CORE, j).wait_recv()
                if j >= LEAD:
                    gather(T_Z, j).wait_recv()

            @pl.when(odd == 0)
            def _():
                for j in range(LEAD):
                    gather(T_Z, j).wait_recv()

            fill_near(0, 2)
    for k in range(CHUNKS):
        gather(I_FWD, k).wait_recv()
    fill_near(2, 4)
    staged[T_Z] = near_texts(1).astype(BF16)

    @pl.when(odd == 1)
    def _():
        for k in range(EARLY):
            back(T_Z, k).start()

    head = rows - part
    for k in range(CHUNKS - 1):
        gather(T_FWD, k).wait_recv()
    fill_far(rows, head)
    staged[T_FWD, pl.ds(0, head)] = far_texts(rows, head).astype(BF16)

    for k in range(CHUNKS - 1):
        back(T_FWD, k).start()

    fill_far(0, rows)
    image_acc[...] = near_images(2, 2) + far_images(2, 2, 0, rows + head)
    text_acc[...] = far_texts(0, rows)
    gather(T_FWD, CHUNKS - 1).wait_recv()

    fill_far(rows + head, part)
    staged[T_FWD, pl.ds(head, part)] = far_texts(rows + head, part).astype(BF16)
    back(T_FWD, CHUNKS - 1).start()
    image_acc[...] = scale * (image_acc[...] + far_images(2, 2, rows + head, part))
    staged[I_FWD] = image_acc[pl.ds(rows, rows)].astype(BF16)
    for k in range(CHUNKS):
        back(I_FWD, k).start()
    for k in range(CHUNKS):
        back(I_FWD, k).wait_recv()
        at = pl.ds(k * part, part)
        staged[I_Y, at] = (image_acc[at] + landed[I_FWD, at].astype(F32)).astype(BF16)
        back(I_Y, k).start()
    for k in range(CHUNKS):
        back(T_FWD, k).wait_recv()
        at = pl.ds(k * part, part)
        staged[T_Y, at] = (text_acc[at] + landed[T_FWD, at].astype(F32)).astype(BF16)
        back(T_Y, k).start()
        if k == CHUNKS - 1 - AHEAD:

            @pl.when(odd == 0)
            def _():
                for j in range(CHUNKS):
                    back(T_Z, j).start()

            @pl.when(odd == 1)
            def _():
                for j in range(EARLY, CHUNKS):
                    back(T_Z, j).start()

    staged[I_CORE] = (scale * (near_images(1, 1) + far_images(1, 1, 0, 2 * rows))).astype(BF16)
    for k in range(CHUNKS):
        back(I_CORE, k).start()
    image_acc[pl.ds(0, rows)] = scale * (near_images(0, 1) + far_images(0, 1, 0, 2 * rows))
    text_acc[...] = near_texts(0)
    for k in range(CHUNKS):
        at = pl.ds(k * part, part)
        back(I_CORE, k).wait_recv()
        image_acc[at] = image_acc[at] + landed[I_CORE, at].astype(F32)
    for k in range(CHUNKS):
        for stream in range(6):
            gather(stream, k).wait_send()
        for stream in (I_CORE, I_FWD, T_FWD):
            back(stream, k).wait_send()
    for k in range(CHUNKS):
        at = pl.ds(k * part, part)
        if k == CHUNKS - 1:
            for j in range(CHUNKS):
                for stream in (I_Y, T_Z, T_Y):
                    back(stream, j).wait_send()
        back(I_Y, k).wait_recv()
        grad_image_ref[at] = (image_acc[at] + landed[I_Y, at].astype(F32)).astype(BF16)
        back(T_Z, k).wait_recv()
        back(T_Y, k).wait_recv()
        grad_text_ref[at] = (text_acc[at] + landed[T_Z, at].astype(F32) + landed[T_Y, at].astype(F32)).astype(BF16)

def write_out(image_ref, text_ref, grad_image_ref, grad_text_ref, sem):
    copies = [
        pltpu.make_async_copy(image_ref, grad_image_ref, sem.at[0]),
        pltpu.make_async_copy(text_ref, grad_text_ref, sem.at[1]),
    ]
    for copy in copies:
        copy.start()
    for copy in copies:
        copy.wait()


def per_device(image_rows, text_rows, logit_scale, logit_bias):
    rows, width = image_rows.shape
    quarter = lax.axis_size("dp") // 4
    shape = jax.ShapeDtypeStruct((rows, width), BF16)
    vmem = pl.BlockSpec(memory_space=pltpu.VMEM)
    hbm = pl.BlockSpec(memory_space=pltpu.HBM)
    smem = pl.BlockSpec(memory_space=pltpu.SMEM)
    dma = pltpu.SemaphoreType.DMA
    sums = pl.pallas_call(
        functools.partial(kernel, quarter, rows),
        out_shape=(pltpu.VMEM((rows, width), BF16), pltpu.VMEM((rows, width), BF16)),
        in_specs=[smem, smem, hbm, hbm],
        out_specs=(vmem, vmem),
        scratch_shapes=[
            pltpu.VMEM((4 * rows, width), BF16),
            pltpu.VMEM((4 * rows, width), BF16),
            pltpu.VMEM((4 * rows, 2 * rows), BF16),
            pltpu.VMEM((2 * rows, 4 * rows), BF16),
            pltpu.VMEM((2 * rows, width), F32),
            pltpu.VMEM((rows, width), F32),
            pltpu.VMEM((6, rows, width), BF16),
            pltpu.VMEM((6, rows, width), BF16),
            dma((6, CHUNKS)),
            dma((6, CHUNKS)),
            dma((6, CHUNKS)),
            dma((6, CHUNKS)),
            dma((2,)),
        ],
        compiler_params=pltpu.CompilerParams(
            collective_id=0, has_side_effects=True, vmem_limit_bytes=48 * 1024 * 1024
        ),
        cost_estimate=pl.CostEstimate(
            flops=6 * rows * rows * 16 * width, bytes_accessed=8 * rows * width, transcendentals=16 * rows * rows
        ),
        name="contrastive",
    )(logit_scale, logit_bias, *(pltpu.with_memory_space_constraint(a, pltpu.HBM) for a in (image_rows, text_rows)))
    return pl.pallas_call(
        write_out,
        out_shape=(shape, shape),
        in_specs=[vmem, vmem],
        out_specs=(hbm, hbm),
        scratch_shapes=[dma((2,))],
        compiler_params=pltpu.CompilerParams(vmem_limit_bytes=4 * 1024 * 1024),
        name="write_out",
    )(*sums)


def solution(mesh):
    split = P(("dp", "rows"), None)
    return jax.shard_map(
        per_device,
        mesh=mesh,
        in_specs=(split, split, P(), P()),
        out_specs=(split, split),
        check_vma=False,
    )
```

```python
import functools

import jax
import jax.numpy as jnp
from jax import lax
from jax.experimental import pallas as pl
from jax.experimental.pallas import tpu as pltpu
from jax.sharding import PartitionSpec as P

MESH = pl.DeviceIdType.MESH
CHUNKS = 4
LEAD = 4
EARLY = 2
AHEAD = 3
F32 = jnp.float32
BF16 = jnp.bfloat16

I_CORE, I_Y, I_FWD, T_Z, T_Y, T_FWD = range(6)


def sigmoid(x):
    return 1.0 / (1.0 + jnp.exp(-x))


def kernel(
    quarter, rows, scale_ref, bias_ref, image_ref, text_ref, grad_image_ref, grad_text_ref,
    images, texts, near, far, image_acc, text_acc, staged, landed,
    send_sem, recv_sem, back_send, back_recv, local_sem,
):
    dp, row = lax.axis_index("dp"), lax.axis_index("rows")
    low = quarter - 2 * quarter * ((dp // quarter) % 2)
    high = 2 * quarter - 4 * quarter * ((dp // (2 * quarter)) % 2)
    to_y2 = {"dp": dp + low, "rows": row}
    to_y6 = {"dp": dp + low + high, "rows": row}
    to_core = {"dp": dp, "rows": row + 1 - 2 * (row % 2)}
    to_z = {"dp": dp, "rows": row + 2 - 4 * (row // 2)}
    partner = {I_CORE: to_core, I_Y: to_y2, I_FWD: to_core, T_Z: to_z, T_Y: to_y6, T_FWD: to_z}
    part = rows // CHUNKS

    load_i = pltpu.make_async_copy(image_ref, images.at[pl.ds(0, rows)], local_sem.at[0])
    load_t = pltpu.make_async_copy(text_ref, texts.at[pl.ds(0, rows)], local_sem.at[1])
    load_i.start()
    load_t.start()
    barrier = pltpu.get_barrier_semaphore()
    for other in (to_y2, to_y6, to_core, to_z):
        pl.semaphore_signal(barrier, inc=1, device_id=other, device_id_type=MESH)
    pl.semaphore_wait(barrier, 4)
    load_i.wait()
    load_t.wait()

    def gather(stream, k):
        held = images if stream < T_Z else texts
        source = {I_CORE: 0, I_Y: 0, I_FWD: 2, T_Z: 0, T_Y: 0, T_FWD: 2}[stream]
        target = {I_CORE: 1, I_Y: 2, I_FWD: 3, T_Z: 1, T_Y: 2, T_FWD: 3}[stream]
        return pltpu.make_async_remote_copy(
            src_ref=held.at[pl.ds(source * rows + k * part, part)],
            dst_ref=held.at[pl.ds(target * rows + k * part, part)],
            send_sem=send_sem.at[stream, k],
            recv_sem=recv_sem.at[stream, k],
            device_id=partner[stream],
            device_id_type=MESH,
        )

    def back(stream, k):
        return pltpu.make_async_remote_copy(
            src_ref=staged.at[stream, pl.ds(k * part, part)],
            dst_ref=landed.at[stream, pl.ds(k * part, part)],
            send_sem=back_send.at[stream, k],
            recv_sem=back_recv.at[stream, k],
            device_id=partner[stream],
            device_id_type=MESH,
        )

    scale = scale_ref[0]
    bias = bias_ref[0]

    def fill_near(i0, i1):
        block = lax.dot_general(
            images[pl.ds(i0 * rows, (i1 - i0) * rows)], texts[pl.ds(0, 2 * rows)], (((1,), (1,)), ((), ())), preferred_element_type=F32
        )
        block = sigmoid(scale * block + bias)
        if i0 == 0:
            r = lax.broadcasted_iota(jnp.int32, block.shape, 0)
            c = lax.broadcasted_iota(jnp.int32, block.shape, 1)
            block = block - jnp.where((r == c) & (r < rows), 1.0, 0.0)
        near[pl.ds(i0 * rows, (i1 - i0) * rows)] = block.astype(BF16)

    def fill_far(start, size):
        block = lax.dot_general(
            texts[pl.ds(2 * rows + start, size)], images[...], (((1,), (1,)), ((), ())), preferred_element_type=F32
        )
        far[pl.ds(start, size)] = sigmoid(scale * block + bias).astype(BF16)

    def near_images(i, n):
        return jnp.dot(near[pl.ds(i * rows, n * rows)], texts[pl.ds(0, 2 * rows)], preferred_element_type=F32)

    def far_images(i, n, start, size):
        return lax.dot_general(
            far[pl.ds(start, size), pl.ds(i * rows, n * rows)],
            texts[pl.ds(2 * rows + start, size)],
            (((0,), (0,)), ((), ())),
            preferred_element_type=F32,
        )

    def near_texts(t):
        return scale * lax.dot_general(
            near[:, pl.ds(t * rows, rows)], images[...], (((0,), (0,)), ((), ())), preferred_element_type=F32
        )

    def far_texts(start, size):
        return scale * jnp.dot(far[pl.ds(start, size)], images[...], preferred_element_type=F32)

    odd = (dp // (quarter // 2)) % 2

    @pl.when(odd == 0)
    def _():
        for k in range(CHUNKS):
            gather(I_Y, k).start()
            gather(T_Y, k).start()

    for k in range(CHUNKS):
        gather(T_Z, k).start()
        gather(I_CORE, k).start()

    @pl.when(odd == 1)
    def _():
        for k in range(LEAD):
            gather(T_Z, k).wait_recv()
        for k in range(CHUNKS):
            gather(I_Y, k).start()
            gather(T_Y, k).start()
    for k in range(CHUNKS):
        gather(I_Y, k).wait_recv()
        gather(I_FWD, k).start()
        gather(T_Y, k).wait_recv()
        gather(T_FWD, k).start()
        if k == CHUNKS - 2:
            for j in range(CHUNKS):
                gather(I_CORE, j).wait_recv()
                if j >= LEAD:
                    gather(T_Z, j).wait_recv()

            @pl.when(odd == 0)
            def _():
                for j in range(LEAD):
                    gather(T_Z, j).wait_recv()

            fill_near(0, 2)
    for k in range(CHUNKS):
        gather(I_FWD, k).wait_recv()
    fill_near(2, 4)
    staged[T_Z] = near_texts(1).astype(BF16)

    @pl.when(odd == 1)
    def _():
        for k in range(EARLY):
            back(T_Z, k).start()

    head = rows - part
    for k in range(CHUNKS - 1):
        gather(T_FWD, k).wait_recv()
    fill_far(rows, head)
    staged[T_FWD, pl.ds(0, head)] = far_texts(rows, head).astype(BF16)

    for k in range(CHUNKS - 1):
        back(T_FWD, k).start()

    fill_far(0, rows)
    image_acc[...] = near_images(2, 2) + far_images(2, 2, 0, rows + head)
    text_acc[...] = far_texts(0, rows)
    gather(T_FWD, CHUNKS - 1).wait_recv()

    fill_far(rows + head, part)
    staged[T_FWD, pl.ds(head, part)] = far_texts(rows + head, part).astype(BF16)
    back(T_FWD, CHUNKS - 1).start()
    image_acc[...] = scale * (image_acc[...] + far_images(2, 2, rows + head, part))
    staged[I_FWD] = image_acc[pl.ds(rows, rows)].astype(BF16)
    for k in range(CHUNKS):
        back(I_FWD, k).start()
    for k in range(CHUNKS):
        back(I_FWD, k).wait_recv()
        at = pl.ds(k * part, part)
        staged[I_Y, at] = (image_acc[at] + landed[I_FWD, at].astype(F32)).astype(BF16)
        back(I_Y, k).start()
    for k in range(CHUNKS):
        back(T_FWD, k).wait_recv()
        at = pl.ds(k * part, part)
        staged[T_Y, at] = (text_acc[at] + landed[T_FWD, at].astype(F32)).astype(BF16)
        back(T_Y, k).start()
        if k == CHUNKS - 1 - AHEAD:

            @pl.when(odd == 0)
            def _():
                for j in range(CHUNKS):
                    back(T_Z, j).start()

            @pl.when(odd == 1)
            def _():
                for j in range(EARLY, CHUNKS):
                    back(T_Z, j).start()

    staged[I_CORE] = (scale * (near_images(1, 1) + far_images(1, 1, 0, 2 * rows))).astype(BF16)
    for k in range(CHUNKS):
        back(I_CORE, k).start()
    image_acc[pl.ds(0, rows)] = scale * (near_images(0, 1) + far_images(0, 1, 0, 2 * rows))
    text_acc[...] = near_texts(0)
    for k in range(CHUNKS):
        at = pl.ds(k * part, part)
        back(I_CORE, k).wait_recv()
        image_acc[at] = image_acc[at] + landed[I_CORE, at].astype(F32)
    for k in range(CHUNKS):
        for stream in range(6):
            gather(stream, k).wait_send()
        for stream in (I_CORE, I_FWD, T_FWD):
            back(stream, k).wait_send()
    for k in range(CHUNKS):
        at = pl.ds(k * part, part)
        if k == CHUNKS - 1:
            for j in range(CHUNKS):
                for stream in (I_Y, T_Z, T_Y):
                    back(stream, j).wait_send()
        back(I_Y, k).wait_recv()
        grad_image_ref[at] = (image_acc[at] + landed[I_Y, at].astype(F32)).astype(BF16)
        back(T_Z, k).wait_recv()
        back(T_Y, k).wait_recv()
        grad_text_ref[at] = (text_acc[at] + landed[T_Z, at].astype(F32) + landed[T_Y, at].astype(F32)).astype(BF16)

def write_out(image_ref, text_ref, grad_image_ref, grad_text_ref, sem):
    copies = [
        pltpu.make_async_copy(image_ref, grad_image_ref, sem.at[0]),
        pltpu.make_async_copy(text_ref, grad_text_ref, sem.at[1]),
    ]
    for copy in copies:
        copy.start()
    for copy in copies:
        copy.wait()


def per_device(image_rows, text_rows, logit_scale, logit_bias):
    rows, width = image_rows.shape
    quarter = lax.axis_size("dp") // 4
    shape = jax.ShapeDtypeStruct((rows, width), BF16)
    vmem = pl.BlockSpec(memory_space=pltpu.VMEM)
    hbm = pl.BlockSpec(memory_space=pltpu.HBM)
    smem = pl.BlockSpec(memory_space=pltpu.SMEM)
    dma = pltpu.SemaphoreType.DMA
    sums = pl.pallas_call(
        functools.partial(kernel, quarter, rows),
        out_shape=(pltpu.VMEM((rows, width), BF16), pltpu.VMEM((rows, width), BF16)),
        in_specs=[smem, smem, hbm, hbm],
        out_specs=(vmem, vmem),
        scratch_shapes=[
            pltpu.VMEM((4 * rows, width), BF16),
            pltpu.VMEM((4 * rows, width), BF16),
            pltpu.VMEM((4 * rows, 2 * rows), BF16),
            pltpu.VMEM((2 * rows, 4 * rows), BF16),
            pltpu.VMEM((2 * rows, width), F32),
            pltpu.VMEM((rows, width), F32),
            pltpu.VMEM((6, rows, width), BF16),
            pltpu.VMEM((6, rows, width), BF16),
            dma((6, CHUNKS)),
            dma((6, CHUNKS)),
            dma((6, CHUNKS)),
            dma((6, CHUNKS)),
            dma((2,)),
        ],
        compiler_params=pltpu.CompilerParams(
            collective_id=0, has_side_effects=True, vmem_limit_bytes=48 * 1024 * 1024
        ),
        cost_estimate=pl.CostEstimate(
            flops=6 * rows * rows * 16 * width, bytes_accessed=8 * rows * width, transcendentals=16 * rows * rows
        ),
        name="contrastive",
    )(logit_scale, logit_bias, *(pltpu.with_memory_space_constraint(a, pltpu.HBM) for a in (image_rows, text_rows)))
    return pl.pallas_call(
        write_out,
        out_shape=(shape, shape),
        in_specs=[vmem, vmem],
        out_specs=(hbm, hbm),
        scratch_shapes=[dma((2,))],
        compiler_params=pltpu.CompilerParams(vmem_limit_bytes=4 * 1024 * 1024),
        name="write_out",
    )(*sums)


def solution(mesh):
    split = P(("dp", "rows"), None)
    return jax.shard_map(
        per_device,
        mesh=mesh,
        in_specs=(split, split, P(), P()),
        out_specs=(split, split),
        check_vma=False,
    )
```
